32 devices in a mesh: outer: 8 (over y, x, core), inner: 4 (over z).
Axes of the slice: x: 2, y: 2, z: 4, core: 2. Of those that a mesh axis runs over, the one named last changes fastest.
Arguments:
- projected: bfloat16 [4096, 12288], P(('outer', 'inner')), may hold values from -6 to 6
- short_taps: float32 [3, 12288], replicated, may hold values from -3 to 3
- rates: float32 [4096, 16], replicated, may hold values from 6.1035156e-05 to 0.05
- residues: float32 [4096, 16], replicated, may hold values from -1.5 to 1.5
- skip_gain: float32 [4096], replicated, may hold values from -4 to 4
Outputs:
- gated: bfloat16 [4096, 4096], P(('outer', 'inner'))
The draws below stay inside these ranges and needn't reach their ends.
All inputs are finite; a program needn't handle non-finite values.
Results may differ from the reference program's by a relative error of at most 0.008.
Values may be sent and summed in bfloat16 or wider, within the bound.
No kernel may reach another device: no remote copies, remote signals or barrier semaphores. Data moves between devices by JAX's collectives and lax.ppermute only.
A program may use at most 128 MiB of HBM per device.

```python
import math
import jax
import jax.numpy as jnp

CH = 4096
MODES = 16
TOKENS = 4096


def shard_levels(key, extent, pieces, least, largest):
    level, own = 1.0, jax.random.fold_in(key, 6)
    for dim, shards_of in pieces:
        draws = jnp.exp(jax.random.uniform(jax.random.fold_in(own, dim), (shards_of,), jnp.float32, least / len(pieces), largest / len(pieces)))
        level = level * jnp.repeat(draws, extent[dim] // shards_of).reshape([-1 if axis == dim else 1 for axis in range(len(extent))])
    return level


def normal_values(stream_key, shape, deviation, reach, pieces=(), dtype=jnp.bfloat16):
    values = deviation * jax.random.normal(stream_key, shape, jnp.float32)
    if pieces:
        values = values * shard_levels(stream_key, shape, pieces, -0.22, 0.18)
    return jnp.clip(values, -reach, reach).astype(dtype)


def setup_inputs(seed: int = 0) -> dict:
    arg_keys = jax.random.split(jax.random.key(seed), 6)
    return {
        "projected": normal_values(arg_keys[0], (TOKENS, 3 * CH), 1.0, 6.0, ((0, 32),)),
        "short_taps": normal_values(arg_keys[1], (3, 3 * CH), 0.5, 3.0, (), jnp.float32),
        "rates": jnp.clip(jnp.exp(jax.random.uniform(arg_keys[2], (CH, MODES), jnp.float32, math.log(6.103515625e-05), math.log(0.05))), 6.103515625e-05, 0.05),
        "residues": normal_values(arg_keys[3], (CH, MODES), MODES ** -0.5, 1.5, (), jnp.float32),
        "skip_gain": normal_values(arg_keys[4], (CH,), 1.0, 4.0, (), jnp.float32),
    }


def reference(projected, short_taps, rates, residues, skip_gain):
    padded = jnp.concatenate([jnp.zeros((2, 3 * CH), jnp.bfloat16), projected], 0).astype(jnp.float32)
    feat = short_taps[0] * padded[2:] + short_taps[1] * padded[1:-1] + short_taps[2] * padded[:-2]
    query = feat[:, :CH]
    key_part = feat[:, CH:2 * CH]
    value = feat[:, 2 * CH:]
    mixed = key_part * value
    times = jnp.arange(TOKENS).astype(jnp.float32)
    filt = jnp.zeros((TOKENS, CH), jnp.float32)
    for mode in range(MODES):
        amplitude = residues[:, mode] * jnp.sqrt(2.0 * rates[:, mode])
        filt = filt + amplitude[None, :] * jnp.exp(-rates[:, mode][None, :] * times[:, None])
    spec_mixed = jnp.fft.rfft(mixed, n=2 * TOKENS, axis=0)
    spec_filt = jnp.fft.rfft(filt, n=2 * TOKENS, axis=0)
    conv = jnp.fft.irfft(spec_mixed * spec_filt, n=2 * TOKENS, axis=0)[:TOKENS]
    return (query * (conv + skip_gain[None, :] * mixed)).astype(jnp.bfloat16)
```

```python
import functools

import jax
import jax.numpy as jnp
from jax import lax
from jax.experimental import pallas as pl
from jax.experimental.pallas import tpu as pltpu
from jax.sharding import PartitionSpec as P

LANES = 128
SUB = 8
AXES = ("outer", "inner")
F32 = jnp.float32
BF16 = jnp.bfloat16


def column(group):
    return pl.ds(pl.multiple_of(group * LANES, LANES), LANES)


def featurize(pad_ref, block_ref, halo_ref, taps_ref, group):
    rows = block_ref.shape[0]
    cols = column(group)
    halo = halo_ref[:, cols].astype(F32)
    pad_ref[SUB - 2 : SUB, :] = halo
    pad_ref[SUB : SUB + rows, :] = block_ref[:, cols].astype(F32)
    taps = taps_ref[:, cols]
    return (
        taps[0:1] * pad_ref[SUB : SUB + rows, :]
        + taps[1:2] * pad_ref[SUB - 1 : SUB - 1 + rows, :]
        + taps[2:3] * pad_ref[SUB - 2 : SUB - 2 + rows, :]
    )


def state_kernel(k_ref, v_ref, hk_ref, hv_ref, tk_ref, tv_ref, rates_ref, mixed_ref, state_ref, pad_k, pad_v):
    rows, width = k_ref.shape
    modes = rates_ref.shape[0]
    place = lax.broadcasted_iota(jnp.int32, (SUB, LANES), 0).astype(F32)

    @pl.loop(0, width // LANES)
    def _(group):
        mixed = featurize(pad_k, k_ref, hk_ref, tk_ref, group) * featurize(
            pad_v, v_ref, hv_ref, tv_ref, group
        )
        mixed_ref[group] = mixed
        rates = rates_ref[:, column(group)]
        for mode in range(modes):
            rate = jnp.broadcast_to(rates[mode : mode + 1], (SUB, LANES))
            stride_decay = jnp.exp(-SUB * rate)
            total = mixed[0:SUB]
            for tile in range(1, rows // SUB):
                total = total * stride_decay + mixed[tile * SUB : (tile + 1) * SUB]
            total = total * jnp.exp(-rate * (SUB - 1 - place))
            state_ref[group, mode : mode + 1, :] = jnp.sum(total, 0, keepdims=True)


def scan_kernel(rows, got_ref, rates_ref, out_ref):
    decay = jnp.exp(-rows * rates_ref[...])

    def step(place, carry):
        out_ref[place] = carry.astype(BF16)
        return carry * decay + got_ref[place].astype(F32)

    lax.fori_loop(0, got_ref.shape[0], step, jnp.zeros(decay.shape, F32), unroll=4)


def local_kernel(mixed_ref, rates_ref, residues_ref, skip_ref, out_ref):
    groups, modes = SUB, rates_ref.shape[0]
    rows = mixed_ref.shape[0] // groups
    rates = [rates_ref[m] for m in range(modes)]
    decays = [jnp.exp(-r) for r in rates]
    gains = [residues_ref[m] * jnp.sqrt(2.0 * rates[m]) for m in range(modes)]
    skip = skip_ref[...]

    def step(token, states):
        at = pl.ds(token, groups, stride=rows)
        x = mixed_ref[at, :]
        states = tuple(s * d + x for s, d in zip(states, decays))
        terms = [s * g for s, g in zip(states, gains)] + [skip * x]
        while len(terms) > 1:
            terms = [a + b for a, b in zip(terms[::2], terms[1::2])] + (
                [terms[-1]] if len(terms) % 2 else []
            )
        out_ref[at, :] = terms[0]
        return states

    lax.fori_loop(0, rows, step, tuple(jnp.zeros((groups, LANES), F32) for _ in range(modes)), unroll=4)


def final_kernel(q_ref, hq_ref, tq_ref, local_ref, carry_ref, rates_ref, residues_ref, out_ref, pad_q):
    rows, width = q_ref.shape
    modes = rates_ref.shape[0]
    place = lax.broadcasted_iota(jnp.int32, (SUB, LANES), 0).astype(F32)

    @pl.loop(0, width // LANES)
    def _(group):
        cols = column(group)
        query = featurize(pad_q, q_ref, hq_ref, tq_ref, group)
        rates = rates_ref[:, cols]
        gains = residues_ref[:, cols] * jnp.sqrt(2.0 * rates) * carry_ref[group].astype(F32)
        strides, terms = [], []
        for mode in range(modes):
            rate = jnp.broadcast_to(rates[mode : mode + 1], (SUB, LANES))
            strides.append(jnp.exp(-SUB * rate))
            terms.append(jnp.exp(-rate * (place + 1.0)) * gains[mode : mode + 1])
        for tile in range(rows // SUB):
            at = slice(tile * SUB, (tile + 1) * SUB)
            level = terms
            while len(level) > 1:
                level = [a + b for a, b in zip(level[::2], level[1::2])] + (
                    [level[-1]] if len(level) % 2 else []
                )
            conv = level[0] + local_ref[group, at, :]
            pad_q[at, :] = query[at] * conv
            terms = [t * s for t, s in zip(terms, strides)]
        out_ref[:, cols] = pad_q[0:rows, :].astype(BF16)


def on_device(projected, short_taps, rates, residues, skip_gain):
    rows, feature_width = projected.shape
    channels = feature_width // 3
    modes = rates.shape[1]
    groups = channels // LANES
    count = lax.axis_size(AXES)
    place = lax.axis_index(AXES)
    own = channels // count
    halo = lax.ppermute(projected[rows - 2 :], AXES, [(s, s + 1) for s in range(count - 1)])
    rates_t, residues_t = rates.T, residues.T

    width = 4 * LANES
    steps = channels // width

    def part(which, height):
        return pl.BlockSpec((height, width), lambda i: (0, which * steps + i))

    by_group = lambda *inner: pl.BlockSpec((width // LANES, *inner), lambda i: (i, 0, 0))
    mixed, state = pl.pallas_call(
        state_kernel,
        grid=(steps,),
        in_specs=[part(1, rows), part(2, rows), part(1, 2), part(2, 2), part(1, 3), part(2, 3), part(0, modes)],
        out_specs=[by_group(rows, LANES), by_group(modes, LANES)],
        out_shape=[
            jax.ShapeDtypeStruct((groups, rows, LANES), F32),
            jax.ShapeDtypeStruct((groups, modes, LANES), F32),
        ],
        scratch_shapes=[pltpu.VMEM((rows + SUB, LANES), F32)] * 2,
        name="state",
    )(projected, projected, halo, halo, short_taps, short_taps, rates_t)

    def to_channels(x):
        x = x.astype(BF16)
        if own != LANES:
            x = jnp.moveaxis(x, 1, 0).reshape(modes, count, own)
            x = jnp.moveaxis(x, 1, 0)
        return x

    def to_groups(x):
        if own != LANES:
            x = jnp.moveaxis(x, 0, 1).reshape(modes, groups, LANES)
            x = jnp.moveaxis(x, 1, 0)
        return x

    got = lax.all_to_all(to_channels(state), AXES, split_axis=0, concat_axis=0, tiled=True)
    own_rates = lax.dynamic_slice_in_dim(rates_t, place * own, own, 1)
    scanned = pl.pallas_call(
        functools.partial(scan_kernel, rows),
        out_shape=jax.ShapeDtypeStruct((count, modes, own), BF16),
        name="scan",
    )(got, own_rates)
    carry = to_groups(lax.all_to_all(scanned, AXES, split_axis=0, concat_axis=0, tiled=True))

    wide = SUB * LANES
    local = pl.pallas_call(
        local_kernel,
        grid=(channels // wide,),
        in_specs=[
            pl.BlockSpec((SUB * rows, LANES), lambda i: (i, 0)),
            pl.BlockSpec((modes, SUB, LANES), lambda i: (0, i, 0)),
            pl.BlockSpec((modes, SUB, LANES), lambda i: (0, i, 0)),
            pl.BlockSpec((SUB, LANES), lambda i: (i, 0)),
        ],
        out_specs=pl.BlockSpec((SUB * rows, LANES), lambda i: (i, 0)),
        out_shape=jax.ShapeDtypeStruct((groups * rows, LANES), F32),
        cost_estimate=pl.CostEstimate(
            flops=4 * modes * rows * channels, bytes_accessed=8 * rows * channels, transcendentals=0
        ),
        name="local",
    )(
        mixed.reshape(groups * rows, LANES),
        rates_t.reshape(modes, groups, LANES),
        residues_t.reshape(modes, groups, LANES),
        skip_gain.reshape(groups, LANES),
    ).reshape(groups, rows, LANES)

    return pl.pallas_call(
        final_kernel,
        grid=(steps,),
        in_specs=[part(0, rows), part(0, 2), part(0, 3), by_group(rows, LANES), by_group(modes, LANES),
                  part(0, modes), part(0, modes)],
        out_specs=pl.BlockSpec((rows, width), lambda i: (0, i)),
        out_shape=jax.ShapeDtypeStruct((rows, channels), BF16),
        scratch_shapes=[pltpu.VMEM((rows + SUB, LANES), F32)],
        name="final",
    )(projected, halo, short_taps, local, carry, rates_t, residues_t)


def solution(mesh):
    in_specs = (P(AXES, None), P(), P(), P(), P())
    out_specs = P(AXES, None)
    return jax.shard_map(
        on_device, mesh=mesh, in_specs=in_specs, out_specs=out_specs, check_vma=False
    )
```

```python
import functools

import jax
import jax.numpy as jnp
from jax import lax
from jax.experimental import pallas as pl
from jax.experimental.pallas import tpu as pltpu
from jax.sharding import PartitionSpec as P

LANES = 128
SUB = 8
PIECES = 4
AXES = ("outer", "inner")
F32 = jnp.float32
BF16 = jnp.bfloat16
HBM = pl.BlockSpec(memory_space=pl.ANY)
VMEM = pl.BlockSpec(memory_space=pltpu.VMEM)
PARAMS = pltpu.CompilerParams(vmem_limit_bytes=32 * 1024 * 1024)


def held(x):
    return pltpu.with_memory_space_constraint(x, pltpu.VMEM)


def column(group):
    return pl.ds(pl.multiple_of(group * LANES, LANES), LANES)


def tree_sum(terms):
    while len(terms) > 1:
        terms = [a + b for a, b in zip(terms[::2], terms[1::2])] + ([terms[-1]] if len(terms) % 2 else [])
    return terms[0]


def short_filter(pad_ref, taps, rows):
    return (
        taps[0:1] * pad_ref[SUB : SUB + rows, :]
        + taps[1:2] * pad_ref[SUB - 1 : SUB - 1 + rows, :]
        + taps[2:3] * pad_ref[SUB - 2 : SUB - 2 + rows, :]
    )


def sublane():
    return lax.broadcasted_iota(jnp.int32, (SUB, LANES), 0)


def state_kernel(proj_ref, taps_hbm, rates_hbm, sent_ref, mixed_ref, k_buf, v_buf, taps_ref, rates_ref, table, ends, pad_k, pad_v, sems, more):
    rows, channels = k_buf.shape
    modes = rates_ref.shape[0]
    groups = channels // LANES
    wide = channels // PIECES
    whole = [pltpu.make_async_copy(rates_hbm, rates_ref, more.at[0]), pltpu.make_async_copy(taps_hbm, taps_ref, more.at[1])]
    pieces = []
    for piece in range(PIECES):
        at = pl.ds(piece * wide, wide)
        pieces.append([
            pltpu.make_async_copy(proj_ref.at[:, pl.ds(channels + piece * wide, wide)], k_buf.at[:, at], sems.at[0, piece]),
            pltpu.make_async_copy(proj_ref.at[:, pl.ds(2 * channels + piece * wide, wide)], v_buf.at[:, at], sems.at[1, piece]),
        ])
    for copy in whole + [c for pair in pieces for c in pair]:
        copy.start()
    whole[0].wait()
    decay = jnp.exp(-rates_ref[...])
    for power in range(4):
        table[power] = decay
        decay = decay * decay
    whole[1].wait()
    row = sublane()
    for piece in range(PIECES):
        for copy in pieces[piece]:
            copy.wait()

        @pl.loop(piece * (groups // PIECES), (piece + 1) * (groups // PIECES))
        def _(group):
            cols = column(group)
            pad_k[SUB : SUB + rows, :] = k_buf[:, cols].astype(F32)
            pad_v[SUB : SUB + rows, :] = v_buf[:, cols].astype(F32)
            mixed = short_filter(pad_k, taps_ref[:, column(groups + group)], rows) * short_filter(
                pad_v, taps_ref[:, column(2 * groups + group)], rows
            )
            tiles = [mixed[i * SUB : (i + 1) * SUB] for i in range(rows // SUB)]
            tiles[0] = jnp.where(row < 2, 0.0, tiles[0])
            for i, tile in enumerate(tiles):
                mixed_ref[pl.ds(pl.multiple_of(group * rows + i * SUB, SUB), SUB), :] = tile
            for mode in range(modes):
                one, two, four, eight = (
                    jnp.broadcast_to(table[power, mode : mode + 1, cols], (SUB, LANES)) for power in range(4)
                )
                total = tiles[0]
                for tile in tiles[1:]:
                    total = total * eight + tile
                total = total + four * pltpu.roll(total, 4, 0)
                total = total + two * pltpu.roll(total, 2, 0)
                total = total + one * pltpu.roll(total, 1, 0)
                ends[mode : mode + 1, :] = total[SUB - 1 :]
            first_k, first_v = pad_k[SUB : 2 * SUB, :], pad_v[SUB : 2 * SUB, :]
            last_k, last_v = pad_k[rows : SUB + rows, :], pad_v[rows : SUB + rows, :]
            ends[modes:, :] = jnp.where(
                row < 2,
                first_k,
                jnp.where(row < 4, pltpu.roll(first_v, 2, 0), jnp.where(row < 6, pltpu.roll(last_k, 6, 0), last_v)),
            )
            sent_ref[group] = ends[...].astype(BF16)


def scan_kernel(rows, modes, got_ref, rates_ref, tk_ref, tv_ref, out_ref):
    one = jnp.exp(-rates_ref[...])
    two = jnp.exp(-2.0 * rates_ref[...])
    rest = jnp.exp(-(rows - 2.0) * rates_ref[...])
    row = sublane()
    taps = [jnp.where(row < 2, tk_ref[i : i + 1, :], tv_ref[i : i + 1, :]) for i in range(3)]

    def step(place, carry):
        state, before = carry
        edge = got_ref[place, modes:, :].astype(F32)
        feat = (
            taps[0] * edge
            + taps[1] * jnp.where(row % 2 == 1, pltpu.roll(edge, 1, 0), pltpu.roll(before, 3, 0))
            + taps[2] * pltpu.roll(before, 4, 0)
        )
        mixed = feat * pltpu.roll(feat, SUB - 2, 0)
        state = state * two + one * mixed[0:1] + mixed[1:2]
        out_ref[place] = state.astype(BF16)
        return state * rest + got_ref[place, :modes, :].astype(F32), edge

    first = (jnp.zeros((modes, LANES), F32), jnp.zeros((SUB, LANES), F32))
    lax.fori_loop(0, got_ref.shape[0], step, first, unroll=8)


def recur(rows, first, blocks, mixed_ref, rates_ref, residues_ref, skip_ref, out_ref):
    modes = rates_ref.shape[0]

    @pl.loop(0, blocks)
    def _(block):
        chosen = pl.ds(pl.multiple_of((first + block) * SUB, SUB), SUB)
        rates = [rates_ref[m, chosen, :] for m in range(modes)]
        decays = [jnp.exp(-r) for r in rates]
        gains = [residues_ref[m, chosen, :] * jnp.sqrt(2.0 * rates[m]) for m in range(modes)]
        skip = skip_ref[chosen, :]

        def step(token, states):
            x = mixed_ref[pl.ds((first + block) * SUB * rows + token, SUB, stride=rows), :]
            states = tuple(s * d + x for s, d in zip(states, decays))
            out_ref[pl.ds(block * SUB * rows + token, SUB, stride=rows), :] = tree_sum(
                [s * g for s, g in zip(states, gains)] + [skip * x]
            )
            return states

        lax.fori_loop(0, rows, step, tuple(jnp.zeros((SUB, LANES), F32) for _ in range(modes)), unroll=4)


def early_kernel(blocks, proj_ref, mixed_ref, rates_ref, residues_ref, skip_ref, out_ref, tail_ref, buf, sem):
    rows = proj_ref.shape[0]
    copy = pltpu.make_async_copy(proj_ref.at[pl.ds(rows - 2 * SUB, 2 * SUB), :], buf, sem)
    copy.start()
    recur(rows, 0, blocks, mixed_ref, rates_ref, residues_ref, skip_ref, out_ref)
    copy.wait()
    tail_ref[...] = buf[2 * SUB - 2 :, :]


def late_kernel(
    first, blocks, proj_ref, halo_ref, after_ref, mixed_ref, rates_ref, residues_ref, skip_ref, taps_ref, flat_rates_ref, flat_residues_ref,
    out_ref, query_ref, start_ref, stride_ref, edge_ref, q_buf, head_buf, pad, sems,
):
    rows, channels = q_buf.shape
    modes = rates_ref.shape[0]
    groups = channels // LANES
    copies = [
        pltpu.make_async_copy(proj_ref.at[:, pl.ds(0, channels)], q_buf, sems.at[0]),
        pltpu.make_async_copy(proj_ref.at[pl.ds(0, 2 * SUB), pl.ds(channels, 2 * channels)], head_buf, sems.at[1]),
    ]
    for copy in copies:
        copy.start()
    recur(rows, first, blocks, mixed_ref, rates_ref, residues_ref, skip_ref, out_ref)
    for copy in copies:
        copy.wait()
    row = sublane()
    place = row.astype(F32) - 1.0

    @pl.loop(0, groups)
    def _(group):
        cols = column(group)
        pad[SUB - 2 : SUB, :] = halo_ref[:, cols].astype(F32)
        pad[SUB : SUB + rows, :] = q_buf[:, cols].astype(F32)
        query_ref[pl.ds(pl.multiple_of(group * rows, rows), rows), :] = short_filter(pad, taps_ref[:, cols], rows)
        rates = flat_rates_ref[:, cols]
        gains = flat_residues_ref[:, cols] * jnp.sqrt(2.0 * rates)
        stride_ref[group] = jnp.exp(-SUB * rates)
        starts = [jnp.exp(-rates[m : m + 1] * place) * gains[m : m + 1] for m in range(modes)]
        for mode in range(modes):
            start_ref[group, mode] = starts[mode]
        mixed = None
        for which in (1, 2):
            at = column(which * groups + group)
            pad[SUB - 2 : SUB, :] = halo_ref[:, at].astype(F32)
            pad[SUB : 3 * SUB, :] = head_buf[:, column((which - 1) * groups + group)].astype(F32)
            feat = short_filter(pad, taps_ref[:, at], SUB)
            mixed = feat if mixed is None else mixed * feat
        skip = skip_ref[pl.ds(group, 1), :]
        own = skip * mixed - jnp.where(row == 0, tree_sum(starts) * pltpu.roll(mixed, SUB - 1, 0), 0.0)
        edge_ref[group] = jnp.where(row < 2, own, 0.0)


def final_kernel(carry_ref, early_ref, late_ref, query_ref, start_ref, stride_ref, edge_ref, out_hbm, out_buf, sems):
    rows, channels = out_buf.shape
    groups, modes = stride_ref.shape[0], stride_ref.shape[1]
    split = early_ref.shape[0] // rows
    copies = []
    for piece in range(PIECES):
        low, high = piece * groups // PIECES, (piece + 1) * groups // PIECES
        local_ref, base = (early_ref, 0) if high <= split else (late_ref, split)

        @pl.loop(low, high)
        def _(group):
            carry = carry_ref[group].astype(F32)
            strides = [jnp.broadcast_to(stride_ref[group, m : m + 1, :], (SUB, LANES)) for m in range(modes)]
            terms = [start_ref[group, m] * carry[m : m + 1] for m in range(modes)]
            made = []
            for tile in range(rows // SUB):
                own = local_ref[pl.ds(pl.multiple_of((group - base) * rows + tile * SUB, SUB), SUB), :]
                if tile == 0:
                    own = own + edge_ref[group]
                query = query_ref[pl.ds(pl.multiple_of(group * rows + tile * SUB, SUB), SUB), :]
                made.append(query * (tree_sum(terms) + own))
                if tile + 1 < rows // SUB:
                    terms = [t * s for t, s in zip(terms, strides)]
            for i in range(0, len(made), 2):
                out_buf[i * SUB : (i + 2) * SUB, column(group)] = jnp.concatenate(made[i : i + 2], 0).astype(BF16)

        at = pl.ds(low * LANES, (high - low) * LANES)
        copies.append(pltpu.make_async_copy(out_buf.at[:, at], out_hbm.at[:, at], sems.at[piece]))
        copies[-1].start()
    for copy in copies:
        copy.wait()


def on_device(projected, short_taps, rates, residues, skip_gain):
    rows, feature_width = projected.shape
    channels = feature_width // 3
    modes = rates.shape[1]
    groups = channels // LANES
    count = lax.axis_size(AXES)
    place = lax.axis_index(AXES)
    own = channels // count
    rates_t, residues_t = rates.T, residues.T
    sent_rows = modes + SUB
    edge_dma = pltpu.SemaphoreType.DMA

    sent, mixed = pl.pallas_call(
        state_kernel,
        in_specs=[HBM, HBM, HBM],
        out_specs=[VMEM, VMEM],
        out_shape=[pltpu.VMEM((groups, sent_rows, LANES), BF16), pltpu.VMEM((groups * rows, LANES), F32)],
        scratch_shapes=[
            pltpu.VMEM((rows, channels), BF16),
            pltpu.VMEM((rows, channels), BF16),
            pltpu.VMEM(short_taps.shape, F32),
            pltpu.VMEM((modes, channels), F32),
            pltpu.VMEM((4, modes, channels), F32),
            pltpu.VMEM((sent_rows, LANES), F32),
            pltpu.VMEM((rows + SUB, LANES), F32),
            pltpu.VMEM((rows + SUB, LANES), F32),
            edge_dma((2, PIECES)),
            edge_dma((2,)),
        ],
        compiler_params=PARAMS,
        name="state",
    )(projected, short_taps, rates_t)

    def exchange(x):
        return lax.all_to_all(x, AXES, split_axis=0, concat_axis=0, tiled=True)

    if own == LANES:
        got = exchange(sent)
    else:
        parts = sent.reshape(groups, sent_rows, LANES // own, own).transpose(0, 2, 1, 3)
        got = exchange(parts.reshape(count, sent_rows, own))
        got = jnp.pad(got, ((0, 0), (0, 0), (0, LANES - own)))

    def own_part(x, start=0):
        part = lax.dynamic_slice_in_dim(x, start + place * own, own, 1)
        return part if own == LANES else jnp.pad(part, ((0, 0), (0, LANES - own)))

    scanned = pl.pallas_call(
        functools.partial(scan_kernel, rows, modes),
        in_specs=[VMEM] * 4,
        out_specs=VMEM,
        out_shape=pltpu.VMEM((count, modes, LANES), BF16),
        compiler_params=PARAMS,
        name="scan",
    )(held(got), own_part(rates_t), own_part(short_taps, channels), own_part(short_taps, 2 * channels))
    if own == LANES:
        carry = exchange(scanned)
    else:
        parts = exchange(scanned[:, :, :own]).reshape(groups, LANES // own, modes, own)
        carry = parts.transpose(0, 2, 1, 3).reshape(groups, modes, LANES)

    by_group = lambda x: x.reshape(modes, groups, LANES)
    skip = skip_gain.reshape(groups, LANES)
    blocks = groups // SUB
    early_blocks = blocks // 2
    early, tail = pl.pallas_call(
        functools.partial(early_kernel, early_blocks),
        in_specs=[HBM, VMEM, VMEM, VMEM, VMEM],
        out_specs=[VMEM, VMEM],
        out_shape=[
            pltpu.VMEM((early_blocks * SUB * rows, LANES), F32),
            pltpu.VMEM((2, feature_width), BF16),
        ],
        scratch_shapes=[pltpu.VMEM((2 * SUB, feature_width), BF16), edge_dma],
        cost_estimate=pl.CostEstimate(flops=2 * modes * rows * channels, bytes_accessed=4 * rows * channels, transcendentals=0),
        compiler_params=PARAMS,
        name="early",
    )(projected, held(mixed), by_group(rates_t), by_group(residues_t), skip)
    halo = lax.ppermute(tail, AXES, [(s, s + 1) for s in range(count - 1)])

    late_blocks = blocks - early_blocks
    late, query, start, stride, edge = pl.pallas_call(
        functools.partial(late_kernel, early_blocks, late_blocks),
        in_specs=[HBM, VMEM, HBM] + [VMEM] * 7,
        out_specs=[VMEM] * 5,
        out_shape=[
            pltpu.VMEM((late_blocks * SUB * rows, LANES), F32),
            pltpu.VMEM((groups * rows, LANES), F32),
            pltpu.VMEM((groups, modes, SUB, LANES), F32),
            pltpu.VMEM((groups, modes, LANES), F32),
            pltpu.VMEM((groups, SUB, LANES), F32),
        ],
        scratch_shapes=[
            pltpu.VMEM((rows, channels), BF16),
            pltpu.VMEM((2 * SUB, 2 * channels), BF16),
            pltpu.VMEM((rows + SUB, LANES), F32),
            edge_dma((2,)),
        ],
        cost_estimate=pl.CostEstimate(flops=2 * modes * rows * channels, bytes_accessed=4 * rows * channels, transcendentals=0),
        compiler_params=PARAMS,
        name="late",
    )(projected, held(halo), scanned, held(mixed), by_group(rates_t), by_group(residues_t), skip, short_taps, rates_t, residues_t)

    return pl.pallas_call(
        final_kernel,
        in_specs=[VMEM] * 7,
        out_specs=HBM,
        out_shape=jax.ShapeDtypeStruct((rows, channels), BF16),
        scratch_shapes=[pltpu.VMEM((rows, channels), BF16), edge_dma((PIECES,))],
        compiler_params=PARAMS,
        name="final",
    )(held(carry), held(early), held(late), held(query), held(start), held(stride), held(edge))


def solution(mesh):
    in_specs = (P(AXES, None), P(), P(), P(), P())
    out_specs = P(AXES, None)
    return jax.shard_map(
        on_device, mesh=mesh, in_specs=in_specs, out_specs=out_specs, check_vma=False
    )
```

```python
import functools

import jax
import jax.numpy as jnp
from jax import lax
from jax.experimental import pallas as pl
from jax.experimental.pallas import tpu as pltpu
from jax.sharding import PartitionSpec as P

LANES = 128
SUB = 8
PIECES = 4
AXES = ("outer", "inner")
F32 = jnp.float32
BF16 = jnp.bfloat16
HBM = pl.BlockSpec(memory_space=pltpu.HBM)
VMEM = pl.BlockSpec(memory_space=pltpu.VMEM)
PARAMS = pltpu.CompilerParams(vmem_limit_bytes=32 * 1024 * 1024)


def held(x):
    return pltpu.with_memory_space_constraint(x, pltpu.VMEM)


def pinned(x):
    return pltpu.with_memory_space_constraint(x, pltpu.HBM)


def column(group):
    return pl.ds(pl.multiple_of(group * LANES, LANES), LANES)


def tree_sum(terms):
    while len(terms) > 1:
        terms = [a + b for a, b in zip(terms[::2], terms[1::2])] + ([terms[-1]] if len(terms) % 2 else [])
    return terms[0]


def short_filter(pad_ref, taps, rows):
    return (
        taps[0:1] * pad_ref[SUB : SUB + rows, :]
        + taps[1:2] * pad_ref[SUB - 1 : SUB - 1 + rows, :]
        + taps[2:3] * pad_ref[SUB - 2 : SUB - 2 + rows, :]
    )


def sublane():
    return lax.broadcasted_iota(jnp.int32, (SUB, LANES), 0)


def state_kernel(proj_ref, taps_hbm, rates_hbm, sent_hbm, mixed_hbm, k_buf, v_buf, taps_ref, rates_ref, table, ends, pad_k, pad_v, sent_ref, mixed_ref, sems, more,
):
    rows, channels = k_buf.shape
    modes = rates_ref.shape[0]
    groups = channels // LANES
    wide = channels // PIECES
    whole = [pltpu.make_async_copy(rates_hbm, rates_ref, more.at[0]), pltpu.make_async_copy(taps_hbm, taps_ref, more.at[1])]
    pieces = []
    for piece in range(PIECES):
        at = pl.ds(piece * wide, wide)
        pieces.append([
            pltpu.make_async_copy(proj_ref.at[:, pl.ds(channels + piece * wide, wide)], k_buf.at[:, at], sems.at[0, piece]),
            pltpu.make_async_copy(proj_ref.at[:, pl.ds(2 * channels + piece * wide, wide)], v_buf.at[:, at], sems.at[1, piece]),
        ])
    for copy in whole + [c for pair in pieces for c in pair]:
        copy.start()
    whole[0].wait()
    decay = jnp.exp(-rates_ref[...])
    for power in range(4):
        table[power] = decay
        decay = decay * decay
    whole[1].wait()
    row = sublane()
    leaving = []
    for piece in range(PIECES):
        for copy in pieces[piece]:
            copy.wait()

        @pl.loop(piece * (groups // PIECES), (piece + 1) * (groups // PIECES))
        def _(group):
            cols = column(group)
            pad_k[SUB : SUB + rows, :] = k_buf[:, cols].astype(F32)
            pad_v[SUB : SUB + rows, :] = v_buf[:, cols].astype(F32)
            mixed = short_filter(pad_k, taps_ref[:, column(groups + group)], rows) * short_filter(
                pad_v, taps_ref[:, column(2 * groups + group)], rows
            )
            tiles = [mixed[i * SUB : (i + 1) * SUB] for i in range(rows // SUB)]
            tiles[0] = jnp.where(row < 2, 0.0, tiles[0])
            for i, tile in enumerate(tiles):
                mixed_ref[pl.ds(pl.multiple_of(group * rows + i * SUB, SUB), SUB), :] = tile
            for mode in range(modes):
                one, two, four, eight = (
                    jnp.broadcast_to(table[power, mode : mode + 1, cols], (SUB, LANES)) for power in range(4)
                )
                total = tiles[0]
                for tile in tiles[1:]:
                    total = total * eight + tile
                total = total + four * pltpu.roll(total, 4, 0)
                total = total + two * pltpu.roll(total, 2, 0)
                total = total + one * pltpu.roll(total, 1, 0)
                ends[mode : mode + 1, :] = total[SUB - 1 :]
            first_k, first_v = pad_k[SUB : 2 * SUB, :], pad_v[SUB : 2 * SUB, :]
            last_k, last_v = pad_k[rows : SUB + rows, :], pad_v[rows : SUB + rows, :]
            ends[modes:, :] = jnp.where(
                row < 2,
                first_k,
                jnp.where(row < 4, pltpu.roll(first_v, 2, 0), jnp.where(row < 6, pltpu.roll(last_k, 6, 0), last_v)),
            )
            sent_ref[group] = ends[...].astype(BF16)

        share = groups // PIECES
        at = pl.ds(piece * share * rows, share * rows)
        leaving.append(pltpu.make_async_copy(mixed_ref.at[at], mixed_hbm.at[at], sems.at[2, piece]))
        at = pl.ds(piece * share, share)
        leaving.append(pltpu.make_async_copy(sent_ref.at[at], sent_hbm.at[at], sems.at[3, piece]))
        for copy in leaving[-2:]:
            copy.start()
    for copy in leaving:
        copy.wait()


def scan_kernel(rows, modes, got_ref, rates_ref, tk_ref, tv_ref, after_ref, out_ref):
    one = jnp.exp(-rates_ref[...])
    two = jnp.exp(-2.0 * rates_ref[...])
    rest = jnp.exp(-(rows - 2.0) * rates_ref[...])
    row = sublane()
    taps = [jnp.where(row < 2, tk_ref[i : i + 1, :], tv_ref[i : i + 1, :]) for i in range(3)]

    def step(place, carry):
        state, before = carry
        edge = got_ref[place, modes:, :].astype(F32)
        feat = (
            taps[0] * edge
            + taps[1] * jnp.where(row % 2 == 1, pltpu.roll(edge, 1, 0), pltpu.roll(before, 3, 0))
            + taps[2] * pltpu.roll(before, 4, 0)
        )
        mixed = feat * pltpu.roll(feat, SUB - 2, 0)
        state = state * two + one * mixed[0:1] + mixed[1:2]
        out_ref[place] = state.astype(BF16)
        return state * rest + got_ref[place, :modes, :].astype(F32), edge

    first = (jnp.zeros((modes, LANES), F32), jnp.zeros((SUB, LANES), F32))
    lax.fori_loop(0, got_ref.shape[0], step, first, unroll=8)


def recur(rows, blocks, mixed_ref, decay_ref, gain_ref, skip_ref, out_ref, before, after):
    modes = decay_ref.shape[0] // (blocks * SUB)
    for block in range(blocks):
        before[block].wait()
        at = [pl.ds((m * blocks + block) * SUB, SUB) for m in range(modes)]
        decays = [decay_ref[a, :] for a in at]
        gains = [gain_ref[a, :] for a in at]
        skip = skip_ref[pl.ds(block * SUB, SUB), :]

        def step(token, states):
            here = pl.ds(block * SUB * rows + token, SUB, stride=rows)
            x = mixed_ref[here, :]
            states = tuple(s * d + x for s, d in zip(states, decays))
            out_ref[here, :] = tree_sum([s * g for s, g in zip(states, gains)] + [skip * x])
            return states

        lax.fori_loop(0, rows, step, tuple(jnp.zeros((SUB, LANES), F32) for _ in range(modes)), unroll=4)
        after[block].start()


def spread(rates_ref, residues_ref, decay_ref, gain_ref, first, groups):
    modes = rates_ref.shape[0]
    for group in range(groups):
        cols = slice((first + group) * LANES, (first + group + 1) * LANES)
        rates = rates_ref[:, cols]
        at = pl.ds(group, modes, stride=groups)
        decay_ref[at, :] = jnp.exp(-rates)
        gain_ref[at, :] = residues_ref[:, cols] * jnp.sqrt(2.0 * rates)


def block_copies(blocks, size, first, from_ref, to_ref, sems):
    copies = []
    for block in range(blocks):
        source = from_ref.at[pl.ds((first + block) * size, size)]
        copies.append(pltpu.make_async_copy(source, to_ref.at[pl.ds(block * size, size)], sems.at[block]))
    return copies


def early_kernel(
    blocks, proj_ref, mixed_hbm, rates_hbm, residues_hbm, skip_hbm, out_hbm, tail_ref,
    buf, mixed_ref, rates_ref, residues_ref, skip_ref, decay_ref, gain_ref, out_ref, sems, in_sems, out_sems,
):
    rows = proj_ref.shape[0]
    copies = [
        pltpu.make_async_copy(rates_hbm, rates_ref, sems.at[0]),
        pltpu.make_async_copy(residues_hbm, residues_ref, sems.at[1]),
        pltpu.make_async_copy(skip_hbm, skip_ref, sems.at[2]),
        pltpu.make_async_copy(proj_ref.at[pl.ds(rows - 2 * SUB, 2 * SUB), :], buf, sems.at[3]),
    ]
    size = SUB * rows
    before = block_copies(blocks, size, 0, mixed_hbm, mixed_ref, in_sems)
    after = block_copies(blocks, size, 0, out_ref, out_hbm, out_sems)
    for copy in copies + before:
        copy.start()
    for copy in copies:
        copy.wait()
    tail_ref[...] = buf[2 * SUB - 2 :, :]
    spread(rates_ref, residues_ref, decay_ref, gain_ref, 0, blocks * SUB)
    recur(rows, blocks, mixed_ref, decay_ref, gain_ref, skip_ref, out_ref, before, after)
    for copy in after:
        copy.wait()


def late_kernel(
    first, blocks, proj_ref, halo_ref, after_ref, mixed_hbm, rates_hbm, residues_hbm, skip_hbm, taps_hbm,
    out_hbm, query_hbm, start_hbm, stride_hbm, edge_hbm,
    q_buf, head_buf, pad, mixed_ref, rates_ref, residues_ref, skip_ref, taps_ref, decay_ref, gain_ref,
    out_ref, query_ref, start_ref, stride_ref, edge_ref, sems, in_sems, out_sems,
):
    rows, channels = q_buf.shape
    modes = rates_ref.shape[0]
    groups = channels // LANES
    copies = [
        pltpu.make_async_copy(rates_hbm, rates_ref, sems.at[0]),
        pltpu.make_async_copy(residues_hbm, residues_ref, sems.at[1]),
        pltpu.make_async_copy(skip_hbm, skip_ref, sems.at[2]),
        pltpu.make_async_copy(taps_hbm, taps_ref, sems.at[3]),
        pltpu.make_async_copy(proj_ref.at[:, pl.ds(0, channels)], q_buf, sems.at[4]),
        pltpu.make_async_copy(proj_ref.at[pl.ds(0, 2 * SUB), pl.ds(channels, 2 * channels)], head_buf, sems.at[5]),
    ]
    size = SUB * rows
    before = block_copies(blocks, size, first, mixed_hbm, mixed_ref, in_sems)
    after = block_copies(blocks, size, 0, out_ref, out_hbm, out_sems)
    for copy in copies + before:
        copy.start()
    for copy in copies:
        copy.wait()
    row = sublane()
    place = row.astype(F32) - 1.0

    @pl.loop(0, groups)
    def _(group):
        cols = column(group)
        pad[SUB - 2 : SUB, :] = halo_ref[:, cols].astype(F32)
        pad[SUB : SUB + rows, :] = q_buf[:, cols].astype(F32)
        query_ref[pl.ds(pl.multiple_of(group * rows, rows), rows), :] = short_filter(pad, taps_ref[:, cols], rows)
        rates = rates_ref[:, cols]
        gains = residues_ref[:, cols] * jnp.sqrt(2.0 * rates)
        stride_ref[group] = jnp.exp(-SUB * rates)
        starts = [jnp.exp(-rates[m : m + 1] * place) * gains[m : m + 1] for m in range(modes)]
        for mode in range(modes):
            start_ref[group, mode] = starts[mode]
        mixed = None
        for which in (1, 2):
            at = column(which * groups + group)
            pad[SUB - 2 : SUB, :] = halo_ref[:, at].astype(F32)
            pad[SUB : 3 * SUB, :] = head_buf[:, column((which - 1) * groups + group)].astype(F32)
            feat = short_filter(pad, taps_ref[:, at], SUB)
            mixed = feat if mixed is None else mixed * feat
        skip = skip_ref[pl.ds(group, 1), :]
        own = skip * mixed - jnp.where(row == 0, tree_sum(starts) * pltpu.roll(mixed, SUB - 1, 0), 0.0)
        edge_ref[group] = jnp.where(row < 2, own, 0.0)

    leaving = [
        pltpu.make_async_copy(query_ref, query_hbm, sems.at[6]),
        pltpu.make_async_copy(start_ref, start_hbm, sems.at[7]),
        pltpu.make_async_copy(stride_ref, stride_hbm, sems.at[8]),
        pltpu.make_async_copy(edge_ref, edge_hbm, sems.at[9]),
    ]
    for copy in leaving:
        copy.start()
    spread(rates_ref, residues_ref, decay_ref, gain_ref, first * SUB, blocks * SUB)
    recur(rows, blocks, mixed_ref, decay_ref, gain_ref, skip_ref.at[pl.ds(first * SUB, blocks * SUB)], out_ref, before, after)
    for copy in leaving + after:
        copy.wait()


def final_kernel(
    carry_ref, early_hbm, late_hbm, query_hbm, start_hbm, stride_hbm, edge_hbm, out_hbm,
    local_ref, query_ref, start_ref, stride_ref, edge_ref, out_buf, sems,
):
    rows, channels = out_buf.shape
    groups, modes = stride_ref.shape[0], stride_ref.shape[1]
    split = early_hbm.shape[0] // rows
    share = groups // PIECES
    arriving = []
    for piece in range(PIECES):
        low = piece * share
        local_hbm, base = (early_hbm, 0) if low + share <= split else (late_hbm, split)
        by_row = pl.ds(low * rows, share * rows)
        by_group = pl.ds(low, share)
        arriving.append([
            pltpu.make_async_copy(start_hbm.at[by_group], start_ref.at[by_group], sems.at[piece, 0]),
            pltpu.make_async_copy(stride_hbm.at[by_group], stride_ref.at[by_group], sems.at[piece, 1]),
            pltpu.make_async_copy(edge_hbm.at[by_group], edge_ref.at[by_group], sems.at[piece, 2]),
            pltpu.make_async_copy(local_hbm.at[pl.ds((low - base) * rows, share * rows)], local_ref.at[by_row], sems.at[piece, 3]),
            pltpu.make_async_copy(query_hbm.at[by_row], query_ref.at[by_row], sems.at[piece, 4]),
        ])
        for copy in arriving[-1]:
            copy.start()
    copies = []
    for piece in range(PIECES):
        low = piece * share
        for copy in arriving[piece]:
            copy.wait()

        @pl.loop(low, low + share)
        def _(group):
            carry = carry_ref[group].astype(F32)
            strides = [jnp.broadcast_to(stride_ref[group, m : m + 1, :], (SUB, LANES)) for m in range(modes)]
            terms = [start_ref[group, m] * carry[m : m + 1] for m in range(modes)]
            made = []
            for tile in range(rows // SUB):
                at = pl.ds(pl.multiple_of(group * rows + tile * SUB, SUB), SUB)
                own = local_ref[at, :]
                if tile == 0:
                    own = own + edge_ref[group]
                made.append(query_ref[at, :] * (tree_sum(terms) + own))
                if tile + 1 < rows // SUB:
                    terms = [t * s for t, s in zip(terms, strides)]
            for i in range(0, len(made), 2):
                out_buf[i * SUB : (i + 2) * SUB, column(group)] = jnp.concatenate(made[i : i + 2], 0).astype(BF16)

        at = pl.ds(low * LANES, share * LANES)
        copies.append(pltpu.make_async_copy(out_buf.at[:, at], out_hbm.at[:, at], sems.at[piece, 5]))
        copies[-1].start()
    for copy in copies:
        copy.wait()


def on_device(projected, short_taps, rates, residues, skip_gain):
    rows, feature_width = projected.shape
    channels = feature_width // 3
    modes = rates.shape[1]
    groups = channels // LANES
    count = lax.axis_size(AXES)
    place = lax.axis_index(AXES)
    own = channels // count
    rates_t, residues_t = rates.T, residues.T
    sent_rows = modes + SUB
    dma = pltpu.SemaphoreType.DMA

    def f32_vmem(*shape):
        return pltpu.VMEM(shape, F32)

    sent, mixed = pl.pallas_call(
        state_kernel,
        in_specs=[HBM, HBM, HBM],
        out_specs=[HBM, HBM],
        out_shape=[pltpu.HBM((groups, sent_rows, LANES), BF16), pltpu.HBM((groups * rows, LANES), F32)],
        scratch_shapes=[
            pltpu.VMEM((rows, channels), BF16),
            pltpu.VMEM((rows, channels), BF16),
            f32_vmem(*short_taps.shape),
            f32_vmem(modes, channels),
            f32_vmem(4, modes, channels),
            f32_vmem(sent_rows, LANES),
            f32_vmem(rows + SUB, LANES),
            f32_vmem(rows + SUB, LANES),
            pltpu.VMEM((groups, sent_rows, LANES), BF16),
            f32_vmem(groups * rows, LANES),
            dma((4, PIECES)),
            dma((2,)),
        ],
        compiler_params=PARAMS,
        name="state",
    )(pinned(projected), pinned(short_taps), pinned(rates_t))

    def exchange(x):
        return lax.all_to_all(x, AXES, split_axis=0, concat_axis=0, tiled=True)

    if own == LANES:
        got = exchange(sent)
    else:
        parts = sent.reshape(groups, sent_rows, LANES // own, own).transpose(0, 2, 1, 3)
        got = exchange(parts.reshape(count, sent_rows, own))
        got = jnp.pad(got, ((0, 0), (0, 0), (0, LANES - own)))

    def own_part(x, start=0):
        part = lax.dynamic_slice_in_dim(x, start + place * own, own, 1)
        return part if own == LANES else jnp.pad(part, ((0, 0), (0, LANES - own)))

    blocks = groups // SUB
    early_blocks = blocks // 2
    late_blocks = blocks - early_blocks
    skip = skip_gain.reshape(groups, LANES)
    cost = pl.CostEstimate(flops=2 * modes * rows * channels, bytes_accessed=4 * rows * channels, transcendentals=0)

    def recur_scratch(count):
        return [
            f32_vmem(modes, channels),
            f32_vmem(modes, channels),
            f32_vmem(groups, LANES),
        ], [
            f32_vmem(count * SUB * modes, LANES),
            f32_vmem(count * SUB * modes, LANES),
            f32_vmem(count * SUB * rows, LANES),
        ]

    params, tables = recur_scratch(early_blocks)
    early, tail = pl.pallas_call(
        functools.partial(early_kernel, early_blocks),
        in_specs=[HBM] * 5,
        out_specs=[HBM, VMEM],
        out_shape=[pltpu.HBM((early_blocks * SUB * rows, LANES), F32), pltpu.VMEM((2, feature_width), BF16)],
        scratch_shapes=[
            pltpu.VMEM((2 * SUB, feature_width), BF16),
            f32_vmem(early_blocks * SUB * rows, LANES),
            *params,
            *tables,
            dma((4,)),
            dma((early_blocks,)),
            dma((early_blocks,)),
        ],
        cost_estimate=cost,
        compiler_params=PARAMS,
        name="early",
    )(pinned(projected), pinned(mixed), pinned(rates_t), pinned(residues_t), pinned(skip))
    halo = lax.ppermute(tail, AXES, [(s, s + 1) for s in range(count - 1)])

    scanned = pl.pallas_call(
        functools.partial(scan_kernel, rows, modes),
        in_specs=[VMEM] * 4 + [HBM],
        out_specs=VMEM,
        out_shape=pltpu.VMEM((count, modes, LANES), BF16),
        compiler_params=PARAMS,
        name="scan",
    )(held(got), own_part(rates_t), own_part(short_taps, channels), own_part(short_taps, 2 * channels), pinned(early))
    if own == LANES:
        carry = exchange(scanned)
    else:
        parts = exchange(scanned[:, :, :own]).reshape(groups, LANES // own, modes, own)
        carry = parts.transpose(0, 2, 1, 3).reshape(groups, modes, LANES)

    params, tables = recur_scratch(late_blocks)
    made = [(groups * rows, LANES), (groups, modes, SUB, LANES), (groups, modes, LANES), (groups, SUB, LANES)]
    late, query, start, stride, edge = pl.pallas_call(
        functools.partial(late_kernel, early_blocks, late_blocks),
        in_specs=[HBM, VMEM] + [HBM] * 6,
        out_specs=[HBM] * 5,
        out_shape=[pltpu.HBM((late_blocks * SUB * rows, LANES), F32)] + [pltpu.HBM(shape, F32) for shape in made],
        scratch_shapes=[
            pltpu.VMEM((rows, channels), BF16),
            pltpu.VMEM((2 * SUB, 2 * channels), BF16),
            f32_vmem(rows + SUB, LANES),
            f32_vmem(late_blocks * SUB * rows, LANES),
            *params,
            f32_vmem(*short_taps.shape),
            *tables,
            *[f32_vmem(*shape) for shape in made],
            dma((10,)),
            dma((late_blocks,)),
            dma((late_blocks,)),
        ],
        cost_estimate=cost,
        compiler_params=PARAMS,
        name="late",
    )(pinned(projected), held(halo), pinned(scanned), pinned(mixed), pinned(rates_t), pinned(residues_t), pinned(skip), pinned(short_taps))

    return pl.pallas_call(
        final_kernel,
        in_specs=[VMEM] + [HBM] * 6,
        out_specs=HBM,
        out_shape=pltpu.HBM((rows, channels), BF16),
        scratch_shapes=[f32_vmem(groups * rows, LANES), *[f32_vmem(*shape) for shape in made], pltpu.VMEM((rows, channels), BF16), dma((PIECES, 6))],
        compiler_params=PARAMS,
        name="final",
    )(held(carry), pinned(early), pinned(late), pinned(query), pinned(start), pinned(stride), pinned(edge))


def solution(mesh):
    in_specs = (P(AXES, None), P(), P(), P(), P())
    out_specs = P(AXES, None)
    return jax.shard_map(
        on_device, mesh=mesh, in_specs=in_specs, out_specs=out_specs, check_vma=False
    )
```
